32 devices in a mesh: role: 4 (over x, core), fsdp: 4 (over z), tp: 2 (over y).
Axes of the slice: x: 2, y: 2, z: 4, core: 2. Of those that a mesh axis runs over, the one named last changes fastest.
Arguments:
- master: float32 [5120, 2, 1024], P(('role', 'fsdp', 'tp')), may hold values from -0.078125 to 0.078125
- gradient: float32 [5120, 2, 1024], P(('role', 'fsdp', 'tp')), may hold values from -6 to 6
- first_moment: float32 [5120, 2, 1024], P(('role', 'fsdp', 'tp')), may hold values from -3 to 3
- second_moment: float32 [5120, 2, 1024], P(('role', 'fsdp', 'tp')), may hold values from 0.001 to 1
- key_gain: bfloat16 [128], replicated, may hold values from 0.099609375 to 1.8984375
- hidden: bfloat16 [64, 48, 5120], P(('role', 'fsdp')), may hold values from -6 to 6
- queries: bfloat16 [64, 48, 64, 128], P(('role', 'fsdp'), None, 'tp'), may hold values from -160 to 160
- key_cache: bfloat16 [64, 8, 192, 128], P(('role', 'fsdp'), 'tp'), may hold values from -6 to 6
- value_cache: bfloat16 [64, 8, 192, 128], P(('role', 'fsdp'), 'tp'), may hold values from -6 to 6
- cache_lengths: int32 [64], P(('role', 'fsdp')), may hold values from 2 to 192, as said below
- tool_lengths: int32 [64], P(('role', 'fsdp')), may hold values from 1 to 48, as said below
Outputs:
- updated_master: float32 [5120, 2, 1024], P(('role', 'fsdp', 'tp'))
- updated_first: float32 [5120, 2, 1024], P(('role', 'fsdp', 'tp'))
- updated_second: float32 [5120, 2, 1024], P(('role', 'fsdp', 'tp'))
- new_entries: bfloat16 [64, 48, 2, 1024], P(('role', 'fsdp'), None, None, 'tp')
- attended: bfloat16 [64, 48, 64, 128], P(('role', 'fsdp'), None, 'tp')
The draws below stay inside these ranges and needn't reach their ends.
Inputs may be any that keep to these rules, and one draw needn't show every extreme that they name: `cache_lengths`: one sequence in every draw has exactly 192 filled slots. `tool_lengths`: one sequence in every draw has a tool result of exactly 48 tokens.
All inputs are finite; a program needn't handle non-finite values.
Results may differ from the reference program's by a relative error of at most 0.0059.
Values may be sent and summed in bfloat16 or wider, within the bound.
No kernel may reach another device: no remote copies, remote signals or barrier semaphores. Data moves between devices by JAX's collectives and lax.ppermute only.
A program may use at most 64 MiB of HBM per device.

```python
import math
import jax
import jax.numpy as jnp
from jax import lax

D = 5120
KVH = 8
HD = 128
GROUP = 8
QH = 64
R = 48
CACHE = 192
SEQS = 64


def joint_draw(key):
    cached = jnp.clip(jax.random.normal(jax.random.fold_in(key, 101), (SEQS, KVH, CACHE, HD), jnp.float32), -6.0, 6.0)
    asked = jnp.clip(jax.random.normal(jax.random.fold_in(key, 102), (SEQS, R, KVH * GROUP, HD), jnp.float32), -6.0, 6.0)
    return (cached, asked)


def draw_key_cache(key, part):
    cached, asked = joint_draw(key)
    return cached.astype(jnp.bfloat16)


def draw_queries(key, part):
    cached, asked = joint_draw(key)
    return asked.astype(jnp.bfloat16)


def draw_cache_lengths(key, part):
    found = jax.random.randint(jax.random.fold_in(key, 201), (SEQS,), 2, CACHE + 1, dtype=jnp.int32)
    lowest = jax.random.randint(jax.random.fold_in(key, 202), (), 0, SEQS, dtype=jnp.int32)
    highest = jax.random.randint(jax.random.fold_in(key, 203), (), 0, SEQS, dtype=jnp.int32)
    found = found.at[lowest].set(2)
    return found.at[highest].set(CACHE)


def draw_tool_lengths(key, part):
    found = jax.random.randint(jax.random.fold_in(key, 301), (SEQS,), 1, R + 1, dtype=jnp.int32)
    highest = jax.random.randint(jax.random.fold_in(key, 302), (), 0, SEQS, dtype=jnp.int32)
    return found.at[highest].set(R)


def level_of(rng, dims, pieces, low, largest):
    factor_of = 1.0
    for axis_at, shards_of in pieces:
        heights = jax.random.uniform(jax.random.fold_in(jax.random.fold_in(rng, 6), axis_at), (shards_of,), jnp.float32, low / len(pieces), largest / len(pieces))
        factor_of = factor_of * jnp.repeat(jnp.exp(heights), dims[axis_at] // shards_of).reshape((-1,) + (1,) * (len(dims) - 1 - axis_at))
    return factor_of


def bell_draw(stream_key, dims, deviation, bound, shards=(), held_as=jnp.bfloat16):
    values = jax.random.normal(stream_key, dims, jnp.float32) * deviation
    if len(shards) > 0:
        values = level_of(stream_key, dims, shards, -0.22, 0.18) * values
    return jnp.clip(values, min=-bound, max=bound).astype(held_as)


def setup_inputs(seed: int = 0) -> dict:
    streams_of = jax.random.split(jax.random.key(seed), 12)
    return {
        "master": bell_draw(streams_of[0], (D, 2, KVH * HD), D ** -0.5, 0.078125, ((0, 32),), jnp.float32),
        "gradient": bell_draw(streams_of[1], (D, 2, KVH * HD), 1.0, 6.0, ((0, 32),), jnp.float32),
        "first_moment": bell_draw(streams_of[2], (D, 2, KVH * HD), 0.2, 3.0, ((0, 32),), jnp.float32),
        "second_moment": jnp.clip(jnp.exp(math.log(1.0) - 6.9077552 * jax.random.uniform(streams_of[3], (D, 2, KVH * HD), jnp.float32) ** level_of(streams_of[3], (D, 2, KVH * HD), ((0, 32),), -0.2, 0.2)), 0.001, 1.0),
        "key_gain": jnp.clip(1.0 + 0.18 * jax.random.normal(streams_of[4], (HD,), jnp.float32), 0.099609375, 1.8984375).astype(jnp.bfloat16),
        "hidden": bell_draw(streams_of[5], (SEQS, R, D), 1.0, 6.0, ((0, 16),)),
        "queries": draw_queries(jax.random.fold_in(streams_of[11], 71), 0),
        "key_cache": draw_key_cache(jax.random.fold_in(streams_of[11], 71), 0),
        "value_cache": bell_draw(streams_of[8], (SEQS, KVH, CACHE, HD), 1.0, 6.0, ((0, 16), (1, 2))),
        "cache_lengths": draw_cache_lengths(jax.random.fold_in(streams_of[11], 71), 0),
        "tool_lengths": draw_tool_lengths(jax.random.fold_in(streams_of[11], 71), 0),
    }


learn_rate = 0.01
decay_rate = 0.1
bias_first = 1.0 - 0.9 ** 10
bias_second = 1.0 - 0.95 ** 10
rope_theta = 1000000.0

def adam_update(master, gradient, first_moment, second_moment):
    moment_one = 0.9 * first_moment + 0.1 * gradient
    moment_two = 0.95 * second_moment + 0.05 * gradient * gradient
    step_size = moment_one / bias_first / (jnp.sqrt(moment_two / bias_second) + 1e-08)
    updated = master * (1.0 - learn_rate * decay_rate) - learn_rate * step_size
    return (updated, moment_one, moment_two)

def rotate_keys(raw_keys, positions, key_gain):
    head_size = raw_keys.shape[-1]
    half_size = head_size // 2
    normed = raw_keys / jnp.sqrt(lax.optimization_barrier(jnp.mean(raw_keys * raw_keys, axis=-1, keepdims=True)) + 1e-06)
    normed = normed * key_gain.astype(jnp.float32)
    inverse = rope_theta ** (-(jnp.arange(half_size, dtype=jnp.float32) * 2.0) / head_size)
    angles = positions.astype(jnp.float32)[:, :, None] * inverse[None, None, :]
    cosine = jnp.cos(angles)[:, :, None, :]
    sine_part = jnp.sin(angles)[:, :, None, :]
    lower_half = normed[..., :half_size]
    upper_half = normed[..., half_size:]
    return jnp.concatenate([lower_half * cosine - upper_half * sine_part, upper_half * cosine + lower_half * sine_part], axis=-1)

def attend(queries, key_cache, value_cache, new_keys, new_values, cache_lengths, tool_lengths):
    sequences, new_rows, qheads, head_size = queries.shape
    groups = key_cache.shape[1]
    cache_size = key_cache.shape[2]
    grouped = queries.reshape(sequences, new_rows, groups, qheads // groups, head_size).astype(jnp.float32)
    score_scale = 1.0 / math.sqrt(head_size)
    cache_score = jnp.einsum('srgah,sgch->sgarc', grouped, key_cache.astype(jnp.float32)) * score_scale
    new_score = jnp.einsum('srgah,sugh->sgaru', grouped, new_keys.astype(jnp.float32)) * score_scale
    cache_mask = (jnp.arange(cache_size, dtype=jnp.int32)[None, :] < cache_lengths[:, None])[:, None, None, None, :]
    causal_mask = (jnp.arange(new_rows, dtype=jnp.int32)[None, :] <= jnp.arange(new_rows, dtype=jnp.int32)[:, None])[None, None, None, :, :]
    cache_score = jnp.where(cache_mask, cache_score, -1e+30)
    new_score = jnp.where(causal_mask, new_score, -1e+30)
    row_max = jnp.maximum(lax.optimization_barrier(jnp.max(cache_score, axis=-1)), lax.optimization_barrier(jnp.max(new_score, axis=-1)))
    cache_exp = jnp.exp(cache_score - row_max[..., None])
    new_exp = jnp.exp(new_score - row_max[..., None])
    denominator = lax.optimization_barrier(jnp.sum(cache_exp, axis=-1)) + lax.optimization_barrier(jnp.sum(new_exp, axis=-1))
    cache_prob = cache_exp.astype(jnp.bfloat16).astype(jnp.float32)
    new_prob = new_exp.astype(jnp.bfloat16).astype(jnp.float32)
    mixed = jnp.einsum('sgarc,sgch->sgarh', cache_prob, value_cache.astype(jnp.float32))
    mixed = mixed + jnp.einsum('sgaru,sugh->sgarh', new_prob, new_values.astype(jnp.float32))
    result = mixed / denominator[..., None]
    result = jnp.transpose(result, (0, 3, 1, 2, 4)).reshape(sequences, new_rows, qheads, head_size)
    live_rows = (jnp.arange(new_rows, dtype=jnp.int32)[None, :] < tool_lengths[:, None])[:, :, None, None]
    return jnp.where(live_rows, result, 0.0).astype(jnp.bfloat16)

def reference(master, gradient, first_moment, second_moment, key_gain, hidden, queries, key_cache, value_cache, cache_lengths, tool_lengths):
    updated, moment_one, moment_two = adam_update(master, gradient, first_moment, second_moment)
    weights = updated.astype(jnp.bfloat16).reshape(D, 2 * KVH * HD)
    tokens = hidden.reshape(SEQS * R, D)
    projected = jnp.dot(tokens, weights, preferred_element_type=jnp.float32).reshape(SEQS, R, 2, KVH, HD)
    positions = cache_lengths[:, None] + jnp.arange(R, dtype=jnp.int32)[None, :]
    new_keys = rotate_keys(projected[:, :, 0], positions, key_gain).astype(jnp.bfloat16)
    new_values = projected[:, :, 1].astype(jnp.bfloat16)
    new_entries = jnp.stack([new_keys.reshape(SEQS, R, KVH * HD), new_values.reshape(SEQS, R, KVH * HD)], axis=2)
    block_size = math.gcd(SEQS, 32)

    def split_view(array):
        return array.reshape((SEQS // block_size, block_size) + array.shape[1:])

    def one_block(members):
        return attend(*members)
    attended = lax.map(one_block, (split_view(queries), split_view(key_cache), split_view(value_cache), split_view(new_keys), split_view(new_values), split_view(cache_lengths), split_view(tool_lengths)))
    attended = attended.reshape(SEQS, R, QH, HD)
    return (updated, moment_one, moment_two, new_entries, attended)
```

```python
import functools
import math

import jax
import jax.numpy as jnp
from jax import lax
from jax.experimental import pallas as pl
from jax.experimental.pallas import tpu as pltpu
from jax.sharding import PartitionSpec as P

learn_rate = 0.01
decay_rate = 0.1
bias_first = 1.0 - 0.9**10
bias_second = 1.0 - 0.95**10
rope_theta = 1000000.0


def adam_update(master, gradient, first_moment, second_moment):
    moment_one = 0.9 * first_moment + 0.1 * gradient
    moment_two = 0.95 * second_moment + 0.05 * gradient * gradient
    step_size = moment_one / bias_first / (jnp.sqrt(moment_two / bias_second) + 1e-08)
    updated = master * (1.0 - learn_rate * decay_rate) - learn_rate * step_size
    return (updated, moment_one, moment_two)


def rotate_keys(raw_keys, positions, key_gain):
    head_size = raw_keys.shape[-1]
    half_size = head_size // 2
    normed = raw_keys / jnp.sqrt(jnp.mean(raw_keys * raw_keys, axis=-1, keepdims=True) + 1e-06)
    normed = normed * key_gain.astype(jnp.float32)
    inverse = rope_theta ** (-(jnp.arange(half_size, dtype=jnp.float32) * 2.0) / head_size)
    angles = positions.astype(jnp.float32)[:, :, None] * inverse[None, None, :]
    cosine = jnp.cos(angles)[:, :, None, :]
    sine_part = jnp.sin(angles)[:, :, None, :]
    lower_half = normed[..., :half_size]
    upper_half = normed[..., half_size:]
    return jnp.concatenate(
        [
            lower_half * cosine - upper_half * sine_part,
            upper_half * cosine + lower_half * sine_part,
        ],
        axis=-1,
    )


def attend(queries, key_cache, value_cache, new_keys, new_values, cache_lengths, tool_lengths):
    sequences, new_rows, qheads, head_size = queries.shape
    groups = key_cache.shape[1]
    cache_size = key_cache.shape[2]
    grouped = queries.reshape(sequences, new_rows, groups, qheads // groups, head_size)
    score_scale = 1.0 / math.sqrt(head_size)
    cache_score = (
        jnp.einsum("srgah,sgch->sgarc", grouped, key_cache, preferred_element_type=jnp.float32)
        * score_scale
    )
    new_score = (
        jnp.einsum("srgah,sugh->sgaru", grouped, new_keys, preferred_element_type=jnp.float32)
        * score_scale
    )
    cache_mask = (jnp.arange(cache_size, dtype=jnp.int32)[None, :] < cache_lengths[:, None])[
        :, None, None, None, :
    ]
    causal_mask = (
        jnp.arange(new_rows, dtype=jnp.int32)[None, :]
        <= jnp.arange(new_rows, dtype=jnp.int32)[:, None]
    )[None, None, None, :, :]
    cache_score = jnp.where(cache_mask, cache_score, -1e30)
    new_score = jnp.where(causal_mask, new_score, -1e30)
    row_max = jnp.maximum(jnp.max(cache_score, axis=-1), jnp.max(new_score, axis=-1))
    cache_exp = jnp.exp(cache_score - row_max[..., None])
    new_exp = jnp.exp(new_score - row_max[..., None])
    denominator = jnp.sum(cache_exp, axis=-1) + jnp.sum(new_exp, axis=-1)
    cache_prob = cache_exp.astype(jnp.bfloat16)
    new_prob = new_exp.astype(jnp.bfloat16)
    mixed = jnp.einsum(
        "sgarc,sgch->sgarh", cache_prob, value_cache, preferred_element_type=jnp.float32
    )
    mixed = mixed + jnp.einsum(
        "sgaru,sugh->sgarh", new_prob, new_values, preferred_element_type=jnp.float32
    )
    result = mixed / denominator[..., None]
    result = jnp.transpose(result, (0, 3, 1, 2, 4)).reshape(sequences, new_rows, qheads, head_size)
    live_rows = (jnp.arange(new_rows, dtype=jnp.int32)[None, :] < tool_lengths[:, None])[
        :, :, None, None
    ]
    return jnp.where(live_rows, result, 0.0).astype(jnp.bfloat16)


def plain_device(
    master,
    gradient,
    first_moment,
    second_moment,
    key_gain,
    hidden,
    queries,
    key_cache,
    value_cache,
    cache_lengths,
    tool_lengths,
):
    updated, moment_one, moment_two = adam_update(master, gradient, first_moment, second_moment)
    weights = updated.astype(jnp.bfloat16)
    sequences, new_rows, model_width = hidden.shape
    row_count = sequences * new_rows
    tokens = hidden.reshape(row_count, model_width)
    groups = key_cache.shape[1]
    head_size = key_cache.shape[3]
    kv_cols = groups * head_size
    tp_count = lax.axis_size("tp")
    own_rows = weights.shape[0]
    split_view = tokens.reshape(row_count, model_width // (tp_count * own_rows), tp_count, own_rows)
    picked = lax.dynamic_slice_in_dim(split_view, lax.axis_index("tp"), 1, 2).reshape(row_count, -1)
    tp_rows = lax.all_gather(weights, ("role", "fsdp"), axis=0, tiled=True)
    partial_value = jnp.dot(
        picked, tp_rows.reshape(tp_rows.shape[0], -1), preferred_element_type=jnp.float32
    )
    projected = lax.psum_scatter(
        partial_value.reshape(row_count, 2, weights.shape[2]), "tp", scatter_dimension=2, tiled=True
    )
    projected = projected.reshape(sequences, new_rows, 2, groups, head_size)
    positions = cache_lengths[:, None] + jnp.arange(new_rows, dtype=jnp.int32)[None, :]
    new_keys = rotate_keys(projected[:, :, 0], positions, key_gain).astype(jnp.bfloat16)
    new_values = projected[:, :, 1].astype(jnp.bfloat16)
    new_entries = jnp.stack(
        [
            new_keys.reshape(sequences, new_rows, kv_cols),
            new_values.reshape(sequences, new_rows, kv_cols),
        ],
        axis=2,
    )
    attended = attend(
        queries, key_cache, value_cache, new_keys, new_values, cache_lengths, tool_lengths
    )
    return (updated, moment_one, moment_two, new_entries, attended)


CORE_SWAP = ((0, 1), (1, 0), (2, 3), (3, 2))
X_SWAP = ((0, 2), (1, 3), (2, 0), (3, 1))
DIAGONAL = ((0, 3), (1, 2), (2, 1), (3, 0))
Z_NEAR = ((0, 1), (1, 0), (2, 3), (3, 2))
Z_FAR = ((0, 2), (2, 0), (1, 3), (3, 1))
Z_MIDDLE = ((1, 2), (2, 1))
Z_ENDS = ((2, 3), (1, 0))
TP_SWAP = ((0, 1), (1, 0))
MASKED = -1e30


def adam_kernel(head_count, m_ref, g_ref, f_ref, s_ref, um_ref, uf_ref, us_ref, own_ref, other_ref):
    here = lax.axis_index("tp")
    gradient = g_ref[...]
    moment_one = 0.9 * f_ref[...] + 0.1 * gradient
    moment_two = 0.95 * s_ref[...] + 0.05 * gradient * gradient
    uf_ref[...] = moment_one
    us_ref[...] = moment_two
    scaled = moment_one * (learn_rate / bias_first)
    root = jnp.sqrt(moment_two * (1.0 / bias_second)) + 1e-08
    um_ref[...] = m_ref[...] * (1.0 - learn_rate * decay_rate) - scaled / root
    rows = own_ref.shape[0]
    stride = um_ref.shape[0] // rows
    for side, out in ((here, own_ref), (1 - here, other_ref)):
        for kind in range(2):
            for head in range(head_count):
                start = (head_count * side + head) * 2 + kind
                part = um_ref[pl.ds(start, rows, stride=stride), :]
                column = (kind * head_count + head) * 128
                out[:, column : column + 128] = part.astype(jnp.bfloat16)


def adam_step(master, gradient, first_moment, second_moment, head_count):
    rows, kinds, width = master.shape
    blocks = width // 128

    def linear(array):
        split = array.reshape(rows, kinds, blocks, 128)
        return split.transpose(0, 2, 1, 3).reshape(rows * kinds * blocks, 128)

    def back(array):
        return array.reshape(rows, blocks, kinds, 128).transpose(0, 2, 1, 3).reshape(rows, kinds, width)

    steps = 5
    step_rows = rows // steps
    flat_spec = pl.BlockSpec((step_rows * kinds * blocks, 128), lambda i: (i, 0))
    flat_shape = jax.ShapeDtypeStruct((rows * kinds * blocks, 128), jnp.float32)
    half = kinds * head_count * 128
    half_spec = pl.BlockSpec((step_rows, half), lambda i: (i, 0))
    half_shape = jax.ShapeDtypeStruct((rows, half), jnp.bfloat16)
    updated, one, two, own, other = pl.pallas_call(
        functools.partial(adam_kernel, head_count),
        out_shape=(flat_shape,) * 3 + (half_shape,) * 2,
        grid=(steps,),
        in_specs=[flat_spec] * 4,
        out_specs=(flat_spec,) * 3 + (half_spec,) * 2,
        cost_estimate=pl.CostEstimate(flops=20 * master.size, bytes_accessed=32 * master.size, transcendentals=0),
        name="adam",
    )(linear(master), linear(gradient), linear(first_moment), linear(second_moment))
    return back(updated), back(one), back(two), own, other


def project_kernel(
    h0, h1, h2, h3, o0, p0, o1, p1, o2, p2, ob, pb, oe, pe, keep_ref, send_ref, held, sems
):
    z = lax.axis_index("fsdp")
    t = lax.axis_index("tp")
    rows = o0.shape[0]
    inner = jnp.logical_or(z == 1, z == 2)

    def copy(ref, layer, side, sem):
        start = pl.multiple_of((layer * 2 + side) * rows, 16)
        return pltpu.make_async_copy(ref, held.at[pl.ds(start, rows)], sems.at[sem])

    near, far, last = z ^ 1, z ^ 2, z ^ 3
    copies = [
        copy(o0, z, t, 0),
        copy(p0, z, 1 - t, 1),
        copy(o1, near, t, 2),
        copy(p1, near, 1 - t, 3),
        copy(o2, far, t, 4),
        copy(p2, far, 1 - t, 5),
    ]
    for each in copies:
        each.start()

    @pl.when(inner)
    def _():
        copy(ob, last, t, 6).start()
        copy(pb, last, 1 - t, 7).start()

    @pl.when(jnp.logical_not(inner))
    def _():
        copy(oe, last, t, 6).start()
        copy(pe, last, 1 - t, 7).start()

    for each in copies:
        each.wait()
    copy(ob, last, t, 6).wait()
    copy(pb, last, 1 - t, 7).wait()
    weights = held[...]
    send_ref[0] = jnp.dot(h1[...], weights, preferred_element_type=jnp.float32)
    send_ref[1] = jnp.dot(h3[...], weights, preferred_element_type=jnp.float32)
    keep_ref[0] = jnp.dot(h0[...], weights, preferred_element_type=jnp.float32)
    keep_ref[1] = jnp.dot(h2[...], weights, preferred_element_type=jnp.float32)


def project(tokens, units):
    count, depth = tokens[0].shape
    width = units[0].shape[1]
    result = jax.ShapeDtypeStruct((2, count, width), jnp.float32)
    whole = pl.BlockSpec(memory_space=pltpu.VMEM)
    return pl.pallas_call(
        project_kernel,
        out_shape=(result, result),
        in_specs=[whole] * 4 + [pl.BlockSpec(memory_space=pl.ANY)] * 10,
        out_specs=(whole, whole),
        scratch_shapes=[pltpu.VMEM((depth, width), jnp.bfloat16), pltpu.SemaphoreType.DMA((8,))],
        compiler_params=pltpu.CompilerParams(vmem_limit_bytes=40 * 1024 * 1024),
        cost_estimate=pl.CostEstimate(
            flops=8 * count * depth * width, bytes_accessed=16 * count * width + 2 * depth * width, transcendentals=0
        ),
        name="project",
    )(*tokens, *units)


def cached_kernel(lengths, q_ref, k_ref, v_ref, out_ref, weight_ref):
    filled = lengths[pl.program_id(0)]
    groups, slots, head_size = k_ref.shape
    new_rows, qheads, _ = q_ref.shape
    share = qheads // groups
    rows = new_rows * share
    scale = 1.0 / math.sqrt(head_size)
    queries = q_ref[...].astype(jnp.float32)
    inside = lax.broadcasted_iota(jnp.int32, (rows, slots), 1) < filled
    lane = lax.broadcasted_iota(jnp.int32, (rows, 128), 1)
    level = jnp.full((rows, 128), MASKED, jnp.float32)
    for g in range(groups):
        asked = queries[:, g * share : (g + 1) * share, :].reshape(rows, head_size).astype(jnp.bfloat16)
        scores = lax.dot_general(
            asked, k_ref[g], (((1,), (1,)), ((), ())), preferred_element_type=jnp.float32
        )
        scores = jnp.where(inside, scores * scale, MASKED)
        top = jnp.max(scores, axis=1, keepdims=True)
        expo = jnp.exp(scores - top)
        total = jnp.sum(expo, axis=1, keepdims=True)
        mixed = jnp.dot(expo.astype(jnp.bfloat16), v_ref[g], preferred_element_type=jnp.float32)
        out_ref[g] = mixed / total
        level = jnp.where(lane == new_rows + g, top + jnp.log(total), level)
    weight_ref[...] = level


def attend_cached(queries, key_cache, value_cache, cache_lengths):
    sequences, new_rows, qheads, head_size = queries.shape
    _, groups, slots, _ = key_cache.shape
    rows = new_rows * (qheads // groups)
    cache_spec = pl.BlockSpec((None, groups, slots, head_size), lambda s, n: (s, 0, 0, 0))
    return pl.pallas_call(
        cached_kernel,
        out_shape=(
            jax.ShapeDtypeStruct((sequences, groups, rows, head_size), jnp.float32),
            jax.ShapeDtypeStruct((sequences, rows, 128), jnp.float32),
        ),
        grid_spec=pltpu.PrefetchScalarGridSpec(
            num_scalar_prefetch=1,
            grid=(sequences,),
            in_specs=[
                pl.BlockSpec((None, new_rows, qheads, head_size), lambda s, n: (s, 0, 0, 0)),
                cache_spec,
                cache_spec,
            ],
            out_specs=(
                pl.BlockSpec((None, groups, rows, head_size), lambda s, n: (s, 0, 0, 0)),
                pl.BlockSpec((None, rows, 128), lambda s, n: (s, 0, 0)),
            ),
        ),
        compiler_params=pltpu.CompilerParams(vmem_limit_bytes=40 * 1024 * 1024),
        cost_estimate=pl.CostEstimate(
            flops=4 * sequences * groups * rows * slots * head_size,
            bytes_accessed=12 * 1024 * 1024,
            transcendentals=sequences * groups * rows * slots,
        ),
        name="attend_cached",
    )(cache_lengths, queries, key_cache, value_cache)


def finish_kernel(
    lengths, gain_ref, cos_ref, sin_ref, a_ref, b_ref, c_ref, q_ref, cached_ref, weight_ref, entry_ref, out_ref
):
    live = lengths[pl.program_id(0)]
    new_rows, qheads, head_size = q_ref.shape
    groups = cached_ref.shape[0]
    share = qheads // groups
    rows = new_rows * share
    half = head_size // 2
    scale = 1.0 / math.sqrt(head_size)
    projected = a_ref[...] + b_ref[...] + c_ref[...].astype(jnp.float32)
    gain = gain_ref[...].astype(jnp.float32)
    cosine, sine = cos_ref[...], sin_ref[...]
    queries = q_ref[...].astype(jnp.float32)
    level = weight_ref[...]
    lane = lax.broadcasted_iota(jnp.int32, (rows, 128), 1)
    token = lax.broadcasted_iota(jnp.int32, (rows, 128), 0) // share
    causal = jnp.logical_and(lane <= token, lane < new_rows)
    shown = token < live
    padding = jnp.zeros((128 - new_rows, head_size), jnp.bfloat16)
    results = []
    for g in range(groups):
        raw = projected[:, g * head_size : (g + 1) * head_size]
        normed = raw / jnp.sqrt(jnp.mean(raw * raw, axis=1, keepdims=True) + 1e-06) * gain
        swapped = jnp.concatenate([normed[:, half:], normed[:, :half]], axis=1)
        key = (normed * cosine + swapped * sine).astype(jnp.bfloat16)
        value = projected[:, (groups + g) * head_size : (groups + g + 1) * head_size].astype(jnp.bfloat16)
        entry_ref[:, 0, g * head_size : (g + 1) * head_size] = key
        entry_ref[:, 1, g * head_size : (g + 1) * head_size] = value
        asked = queries[:, g * share : (g + 1) * share, :].reshape(rows, head_size).astype(jnp.bfloat16)
        scores = lax.dot_general(
            asked,
            jnp.concatenate([key, padding], axis=0),
            (((1,), (1,)), ((), ())),
            preferred_element_type=jnp.float32,
        )
        kept = jnp.where(lane == new_rows + g, level, MASKED)
        scores = jnp.where(causal, scores * scale, kept)
        expo = jnp.exp(scores - jnp.max(scores, axis=1, keepdims=True))
        total = jnp.sum(expo, axis=1, keepdims=True)
        mixed = jnp.dot(
            expo.astype(jnp.bfloat16), jnp.concatenate([value, padding], axis=0), preferred_element_type=jnp.float32
        )
        mixed = (mixed + expo[:, new_rows + g : new_rows + g + 1] * cached_ref[g]) / total
        results.append(jnp.where(shown, mixed, 0.0).reshape(new_rows, share, head_size))
    out_ref[...] = jnp.concatenate(results, axis=1).astype(jnp.bfloat16)


def finish(tool_lengths, key_gain, cosine, sine, parts, queries, cached, weight):
    sequences, new_rows, qheads, head_size = queries.shape
    _, groups, rows, _ = cached.shape
    width = parts[0].shape[1]
    row_spec = pl.BlockSpec((new_rows, width), lambda s, n: (s, 0))
    angle_spec = pl.BlockSpec((new_rows, head_size), lambda s, n: (s, 0))
    query_spec = pl.BlockSpec((None, new_rows, qheads, head_size), lambda s, n: (s, 0, 0, 0))
    return pl.pallas_call(
        finish_kernel,
        out_shape=(
            jax.ShapeDtypeStruct((sequences, new_rows, 2, width // 2), jnp.bfloat16),
            jax.ShapeDtypeStruct(queries.shape, jnp.bfloat16),
        ),
        grid_spec=pltpu.PrefetchScalarGridSpec(
            num_scalar_prefetch=1,
            grid=(sequences,),
            in_specs=[
                pl.BlockSpec((1, head_size), lambda s, n: (0, 0)),
                angle_spec,
                angle_spec,
                row_spec,
                row_spec,
                row_spec,
                query_spec,
                pl.BlockSpec((None, groups, rows, head_size), lambda s, n: (s, 0, 0, 0)),
                pl.BlockSpec((None, rows, 128), lambda s, n: (s, 0, 0)),
            ],
            out_specs=(
                pl.BlockSpec((None, new_rows, 2, width // 2), lambda s, n: (s, 0, 0, 0)),
                query_spec,
            ),
        ),
        compiler_params=pltpu.CompilerParams(vmem_limit_bytes=40 * 1024 * 1024),
        name="finish",
    )(tool_lengths, key_gain.reshape(1, head_size), cosine, sine, *parts, queries, cached, weight)


def fast_device(
    master,
    gradient,
    first_moment,
    second_moment,
    key_gain,
    hidden,
    queries,
    key_cache,
    value_cache,
    cache_lengths,
    tool_lengths,
):
    sequences, new_rows, model_width = hidden.shape
    groups, head_size = key_cache.shape[1], key_cache.shape[3]
    count = sequences * new_rows
    tokens = hidden.reshape(count, model_width)
    role = lax.axis_index("role")
    depth = model_width // lax.axis_size("role")

    def block(index):
        return lax.dynamic_slice_in_dim(tokens, index * depth, depth, 1)

    blocks = [
        block(role),
        lax.ppermute(block(role ^ 1), "role", CORE_SWAP),
        lax.ppermute(block(role ^ 2), "role", X_SWAP),
        lax.ppermute(block(role ^ 3), "role", DIAGONAL),
    ]
    updated, moment_one, moment_two, own, other = adam_step(
        master, gradient, first_moment, second_moment, groups
    )
    swapped = lax.ppermute(other, "tp", TP_SWAP)
    units = [own, swapped]
    far = [lax.ppermute(unit, "fsdp", Z_FAR) for unit in units]
    near = [lax.ppermute(unit, "fsdp", Z_NEAR) for unit in units]
    ends = [lax.ppermute(unit, "fsdp", Z_ENDS) for unit in far]
    middle = [lax.ppermute(unit, "fsdp", Z_MIDDLE) for unit in units]
    keep, send = project(blocks, units + near + far + middle + ends)
    crossed = lax.ppermute(send, "role", CORE_SWAP)
    outgoing = (keep[1] + crossed[1]).astype(jnp.bfloat16)
    arrived = lax.ppermute(outgoing, "role", X_SWAP)

    positions = (cache_lengths[:, None] + jnp.arange(new_rows, dtype=jnp.int32)[None, :]).reshape(count)
    half = head_size // 2
    inverse = rope_theta ** (-(jnp.arange(half, dtype=jnp.float32) * 2.0) / head_size)
    angles = positions.astype(jnp.float32)[:, None] * inverse[None, :]
    cosine, sine = jnp.cos(angles), jnp.sin(angles)
    cosine = jnp.concatenate([cosine, cosine], axis=1)
    sine = jnp.concatenate([-sine, sine], axis=1)
    cached, weight = attend_cached(queries, key_cache, value_cache, cache_lengths)
    new_entries, attended = finish(
        tool_lengths,
        key_gain,
        cosine,
        sine,
        (keep[0], crossed[0], arrived),
        queries,
        cached,
        weight,
    )
    return (updated, moment_one, moment_two, new_entries, attended)


def device_program(mesh):
    sizes = (mesh.shape["role"], mesh.shape["fsdp"], mesh.shape["tp"])
    return fast_device if sizes == (4, 4, 2) else plain_device


def solution(mesh):
    return jax.shard_map(
        device_program(mesh),
        mesh=mesh,
        in_specs=(
            P(("role", "fsdp", "tp"), None, None),
            P(("role", "fsdp", "tp"), None, None),
            P(("role", "fsdp", "tp"), None, None),
            P(("role", "fsdp", "tp"), None, None),
            P(),
            P(("role", "fsdp"), None, None),
            P(("role", "fsdp"), None, "tp", None),
            P(("role", "fsdp"), "tp", None, None),
            P(("role", "fsdp"), "tp", None, None),
            P(("role", "fsdp")),
            P(("role", "fsdp")),
        ),
        out_specs=(
            P(("role", "fsdp", "tp"), None, None),
            P(("role", "fsdp", "tp"), None, None),
            P(("role", "fsdp", "tp"), None, None),
            P(("role", "fsdp"), None, None, "tp"),
            P(("role", "fsdp"), None, "tp", None),
        ),
        check_vma=False,
    )
```

```python
import functools
import math

import jax
import jax.numpy as jnp
from jax import lax
from jax.experimental import pallas as pl
from jax.experimental.pallas import tpu as pltpu
from jax.sharding import PartitionSpec as P

learn_rate = 0.01
decay_rate = 0.1
bias_first = 1.0 - 0.9**10
bias_second = 1.0 - 0.95**10
rope_theta = 1000000.0


def adam_update(master, gradient, first_moment, second_moment):
    moment_one = 0.9 * first_moment + 0.1 * gradient
    moment_two = 0.95 * second_moment + 0.05 * gradient * gradient
    step_size = moment_one / bias_first / (jnp.sqrt(moment_two / bias_second) + 1e-08)
    updated = master * (1.0 - learn_rate * decay_rate) - learn_rate * step_size
    return (updated, moment_one, moment_two)


def rotate_keys(raw_keys, positions, key_gain):
    head_size = raw_keys.shape[-1]
    half_size = head_size // 2
    normed = raw_keys / jnp.sqrt(jnp.mean(raw_keys * raw_keys, axis=-1, keepdims=True) + 1e-06)
    normed = normed * key_gain.astype(jnp.float32)
    inverse = rope_theta ** (-(jnp.arange(half_size, dtype=jnp.float32) * 2.0) / head_size)
    angles = positions.astype(jnp.float32)[:, :, None] * inverse[None, None, :]
    cosine = jnp.cos(angles)[:, :, None, :]
    sine_part = jnp.sin(angles)[:, :, None, :]
    lower_half = normed[..., :half_size]
    upper_half = normed[..., half_size:]
    return jnp.concatenate(
        [
            lower_half * cosine - upper_half * sine_part,
            upper_half * cosine + lower_half * sine_part,
        ],
        axis=-1,
    )


def attend(queries, key_cache, value_cache, new_keys, new_values, cache_lengths, tool_lengths):
    sequences, new_rows, qheads, head_size = queries.shape
    groups = key_cache.shape[1]
    cache_size = key_cache.shape[2]
    grouped = queries.reshape(sequences, new_rows, groups, qheads // groups, head_size)
    score_scale = 1.0 / math.sqrt(head_size)
    cache_score = (
        jnp.einsum("srgah,sgch->sgarc", grouped, key_cache, preferred_element_type=jnp.float32)
        * score_scale
    )
    new_score = (
        jnp.einsum("srgah,sugh->sgaru", grouped, new_keys, preferred_element_type=jnp.float32)
        * score_scale
    )
    cache_mask = (jnp.arange(cache_size, dtype=jnp.int32)[None, :] < cache_lengths[:, None])[
        :, None, None, None, :
    ]
    causal_mask = (
        jnp.arange(new_rows, dtype=jnp.int32)[None, :]
        <= jnp.arange(new_rows, dtype=jnp.int32)[:, None]
    )[None, None, None, :, :]
    cache_score = jnp.where(cache_mask, cache_score, -1e30)
    new_score = jnp.where(causal_mask, new_score, -1e30)
    row_max = jnp.maximum(jnp.max(cache_score, axis=-1), jnp.max(new_score, axis=-1))
    cache_exp = jnp.exp(cache_score - row_max[..., None])
    new_exp = jnp.exp(new_score - row_max[..., None])
    denominator = jnp.sum(cache_exp, axis=-1) + jnp.sum(new_exp, axis=-1)
    cache_prob = cache_exp.astype(jnp.bfloat16)
    new_prob = new_exp.astype(jnp.bfloat16)
    mixed = jnp.einsum(
        "sgarc,sgch->sgarh", cache_prob, value_cache, preferred_element_type=jnp.float32
    )
    mixed = mixed + jnp.einsum(
        "sgaru,sugh->sgarh", new_prob, new_values, preferred_element_type=jnp.float32
    )
    result = mixed / denominator[..., None]
    result = jnp.transpose(result, (0, 3, 1, 2, 4)).reshape(sequences, new_rows, qheads, head_size)
    live_rows = (jnp.arange(new_rows, dtype=jnp.int32)[None, :] < tool_lengths[:, None])[
        :, :, None, None
    ]
    return jnp.where(live_rows, result, 0.0).astype(jnp.bfloat16)


def plain_device(
    master,
    gradient,
    first_moment,
    second_moment,
    key_gain,
    hidden,
    queries,
    key_cache,
    value_cache,
    cache_lengths,
    tool_lengths,
):
    updated, moment_one, moment_two = adam_update(master, gradient, first_moment, second_moment)
    weights = updated.astype(jnp.bfloat16)
    sequences, new_rows, model_width = hidden.shape
    row_count = sequences * new_rows
    tokens = hidden.reshape(row_count, model_width)
    groups = key_cache.shape[1]
    head_size = key_cache.shape[3]
    kv_cols = groups * head_size
    tp_count = lax.axis_size("tp")
    own_rows = weights.shape[0]
    split_view = tokens.reshape(row_count, model_width // (tp_count * own_rows), tp_count, own_rows)
    picked = lax.dynamic_slice_in_dim(split_view, lax.axis_index("tp"), 1, 2).reshape(row_count, -1)
    tp_rows = lax.all_gather(weights, ("role", "fsdp"), axis=0, tiled=True)
    partial_value = jnp.dot(
        picked, tp_rows.reshape(tp_rows.shape[0], -1), preferred_element_type=jnp.float32
    )
    projected = lax.psum_scatter(
        partial_value.reshape(row_count, 2, weights.shape[2]), "tp", scatter_dimension=2, tiled=True
    )
    projected = projected.reshape(sequences, new_rows, 2, groups, head_size)
    positions = cache_lengths[:, None] + jnp.arange(new_rows, dtype=jnp.int32)[None, :]
    new_keys = rotate_keys(projected[:, :, 0], positions, key_gain).astype(jnp.bfloat16)
    new_values = projected[:, :, 1].astype(jnp.bfloat16)
    new_entries = jnp.stack(
        [
            new_keys.reshape(sequences, new_rows, kv_cols),
            new_values.reshape(sequences, new_rows, kv_cols),
        ],
        axis=2,
    )
    attended = attend(
        queries, key_cache, value_cache, new_keys, new_values, cache_lengths, tool_lengths
    )
    return (updated, moment_one, moment_two, new_entries, attended)


CORE_SWAP = ((0, 1), (1, 0), (2, 3), (3, 2))
X_SWAP = ((0, 2), (1, 3), (2, 0), (3, 1))
DIAGONAL = ((0, 3), (1, 2), (2, 1), (3, 0))
XY_SWAP = tuple((2 * r + t, 2 * (r ^ 2) + 1 - t) for r in range(4) for t in range(2))
Z_NEAR = ((0, 1), (1, 0), (2, 3), (3, 2))
Z_FAR = ((0, 2), (2, 0), (1, 3), (3, 1))
Z_MIDDLE = ((1, 2), (2, 1))
Z_ENDS = ((2, 3), (1, 0))
TP_SWAP = ((0, 1), (1, 0))
MASKED = -1e30
QUICK = pl.CostEstimate(flops=1, bytes_accessed=1, transcendentals=0)
VMEM_LIMIT = 60 * 1024 * 1024
ANY = pl.BlockSpec(memory_space=pl.ANY)
VMEM = pl.BlockSpec(memory_space=pltpu.VMEM)


def hold(value, *others):
    return lax.optimization_barrier((value, others))[0]


def adam_kernel(
    chunks, m_ref, g_ref, f_ref, s_ref, um_ref, uf_ref, us_ref, q0, q1, q2, q3, m_buf, g_buf, f_buf, s_buf, in_sem, out_sem
):
    here = lax.axis_index("tp")
    x = lax.axis_index("role") // 2
    size = m_ref.shape[0] // chunks
    rows = q0.shape[0] // chunks
    heads = q0.shape[1] // 256
    ins = ((m_ref, m_buf), (g_ref, g_buf), (f_ref, f_buf), (s_ref, s_buf))
    outs = ((m_buf, um_ref), (f_buf, uf_ref), (s_buf, us_ref))

    def span(c):
        return pl.ds(pl.multiple_of(c * size, size), size)

    def load(c, i):
        return pltpu.make_async_copy(ins[i][0].at[span(c)], ins[i][1].at[span(c)], in_sem.at[c, i])

    def save(c, i):
        return pltpu.make_async_copy(outs[i][0].at[span(c)], outs[i][1].at[span(c)], out_sem.at[c, i])

    for c in range(chunks):
        for i in range(4):
            load(c, i).start()

    def one_chunk(c, _):
        for i in range(4):
            load(c, i).wait()
        base = pl.multiple_of(c * size, size)
        at = span(c)
        gradient = g_buf[at]
        moment_one = 0.9 * f_buf[at] + 0.1 * gradient
        moment_two = 0.95 * s_buf[at] + 0.05 * gradient * gradient
        scaled = moment_one * (learn_rate / bias_first)
        root = jnp.sqrt(moment_two * (1.0 / bias_second)) + 1e-08
        m_buf[at] = m_buf[at] * (1.0 - learn_rate * decay_rate) - scaled / root
        f_buf[at] = moment_one
        s_buf[at] = moment_two
        target = pl.ds(pl.multiple_of(c * rows, rows), rows)
        for side, half, out in ((here, x, q0), (here, 1 - x, q1), (1 - here, x, q2), (1 - here, 1 - x, q3)):
            for kind in range(2):
                for head in range(heads):
                    start = base + (2 * heads * side + heads * half + head) * 2 + kind
                    part = m_buf[pl.ds(start, rows, stride=size // rows), :]
                    column = (kind * heads + head) * 128
                    out[target, column : column + 128] = part.astype(jnp.bfloat16)
        for i in range(3):
            save(c, i).start()
        return 0

    lax.fori_loop(0, chunks, one_chunk, 0)

    def drain(c, _):
        for i in range(3):
            save(c, i).wait()
        return 0

    lax.fori_loop(0, chunks, drain, 0)


def adam_step(master, gradient, first_moment, second_moment):
    rows, kinds, width = master.shape
    blocks = width // 128
    chunks = 5

    def linear(array):
        split = array.reshape(rows, kinds, blocks, 128)
        return split.transpose(0, 2, 1, 3).reshape(rows * kinds * blocks, 128)

    def back(array):
        return array.reshape(rows, blocks, kinds, 128).transpose(0, 2, 1, 3).reshape(rows, kinds, width)

    flat = jax.ShapeDtypeStruct((rows * kinds * blocks, 128), jnp.float32)
    quarter = jax.ShapeDtypeStruct((rows, kinds * width // 4), jnp.bfloat16)
    buffer = pltpu.VMEM(flat.shape, jnp.float32)
    result = pl.pallas_call(
        functools.partial(adam_kernel, chunks),
        out_shape=(flat,) * 3 + (quarter,) * 4,
        in_specs=[ANY] * 4,
        out_specs=(ANY,) * 3 + (VMEM,) * 4,
        scratch_shapes=[buffer] * 4 + [pltpu.SemaphoreType.DMA((chunks, 4)), pltpu.SemaphoreType.DMA((chunks, 3))],
        compiler_params=pltpu.CompilerParams(vmem_limit_bytes=VMEM_LIMIT),
        cost_estimate=QUICK,
        name="adam",
    )(linear(master), linear(gradient), linear(first_moment), linear(second_moment))
    return [back(each) for each in result[:3]], result[3:]


def cut_kernel(tokens, near_ref, far_ref, core_ref, sems):
    core = lax.axis_index("role") % 2
    side = lax.axis_index("tp")
    depth = near_ref.shape[1]
    moves = (
        (2 * side + core, near_ref),
        (2 * side + 1 - core, far_ref),
        (1 - core, core_ref.at[0]),
        (3 - core, core_ref.at[1]),
    )
    copies = []
    for n, (index, out) in enumerate(moves):
        columns = pl.ds(pl.multiple_of(index * depth, 128), depth)
        copies.append(pltpu.make_async_copy(tokens.at[:, columns], out, sems.at[n]))
    for each in copies:
        each.start()
    for each in copies:
        each.wait()


def cut(tokens, depth):
    count = tokens.shape[0]
    one = jax.ShapeDtypeStruct((count, depth), tokens.dtype)
    return pl.pallas_call(
        cut_kernel,
        out_shape=(one, one, jax.ShapeDtypeStruct((2, count, depth), tokens.dtype)),
        in_specs=[ANY],
        out_specs=(VMEM,) * 3,
        scratch_shapes=[pltpu.SemaphoreType.DMA((4,))],
        compiler_params=pltpu.CompilerParams(vmem_limit_bytes=6 * 1024 * 1024),
        cost_estimate=pl.CostEstimate(flops=1, bytes_accessed=8 * 2**20, transcendentals=0),
        name="cut",
    )(tokens)


def project_kernel(
    tokens, c, xa, xb, da, db, o0, p0, o1, p1, o2, p2, om, pm, oe, pe, keep_ref, send_ref, held, h_buf, sems
):
    z = lax.axis_index("fsdp")
    x = lax.axis_index("role") // 2
    core = lax.axis_index("role") % 2
    t = lax.axis_index("tp")
    rows = o0.shape[0]
    depth = xa.shape[1]
    loads = []
    for n in range(2):
        columns = pl.ds(pl.multiple_of((2 * n + core) * depth, 128), depth)
        loads.append(pltpu.make_async_copy(tokens.at[:, columns], h_buf.at[n], sems.at[n]))
    for each in loads:
        each.start()

    def put(value, layer, flip_x, flip_t):
        start = pl.multiple_of((((x ^ flip_x) * 4 + layer) * 2 + (t ^ flip_t)) * rows, 16)
        held[pl.ds(start, rows)] = value

    def group(own, others, layer):
        put(own[...], layer, 0, 0)
        put(others[0], layer, 1, 0)
        put(others[1], layer, 0, 1)
        put(others[2], layer, 1, 1)

    group(o0, p0, z)
    group(o1, p1, z ^ 1)
    group(o2, p2, z ^ 2)
    inner = jnp.logical_or(z == 1, z == 2)

    @pl.when(inner)
    def _():
        group(om, pm, z ^ 3)

    @pl.when(jnp.logical_not(inner))
    def _():
        group(oe, pe, z ^ 3)

    upper, lower = held[:depth], held[depth:]
    a_rows = held[pl.ds(pl.multiple_of(t * depth, 16), depth)]
    b_rows = held[pl.ds(pl.multiple_of((1 - t) * depth, 16), depth)]

    def pair(left, top, right, bottom):
        return jnp.dot(left, top, preferred_element_type=jnp.float32) + jnp.dot(
            right, bottom, preferred_element_type=jnp.float32
        )

    send_ref[0] = pair(c[0], upper, c[1], lower)
    send_ref[1] = pair(da[...], a_rows, db[...], b_rows)
    keep_ref[1] = pair(xa[...], a_rows, xb[...], b_rows)
    for each in loads:
        each.wait()
    keep_ref[0] = pair(h_buf[0], upper, h_buf[1], lower)


def project(tokens, parts, units):
    count, depth = parts[1].shape
    width = units[0].shape[1]
    result = jax.ShapeDtypeStruct((2, count, width), jnp.float32)
    return pl.pallas_call(
        project_kernel,
        out_shape=(result, result),
        in_specs=[ANY] + [VMEM] * (len(parts) + len(units)),
        out_specs=(VMEM, VMEM),
        scratch_shapes=[
            pltpu.VMEM((2 * depth, width), jnp.bfloat16),
            pltpu.VMEM((2, count, depth), jnp.bfloat16),
            pltpu.SemaphoreType.DMA((2,)),
        ],
        compiler_params=pltpu.CompilerParams(vmem_limit_bytes=16 * 1024 * 1024),
        cost_estimate=QUICK,
        name="project",
    )(tokens, *parts, *units)


def rotate_kernel(gain_ref, cos_ref, sin_ref, keep_ref, crossed_ref, own_ref, sent_ref):
    head_size = gain_ref.shape[1]
    half = head_size // 2
    heads = own_ref.shape[1] // (2 * head_size)
    gain = gain_ref[...].astype(jnp.float32)
    for n, out in ((1, sent_ref), (0, own_ref)):
        summed = keep_ref[n] + crossed_ref[n]
        for g in range(heads):
            raw = summed[:, g * head_size : (g + 1) * head_size]
            normed = raw / jnp.sqrt(jnp.mean(raw * raw, axis=1, keepdims=True) + 1e-06) * gain
            swapped = jnp.concatenate([normed[:, half:], normed[:, :half]], axis=1)
            key = normed * cos_ref[n] + swapped * sin_ref[n]
            out[:, g * head_size : (g + 1) * head_size] = key.astype(jnp.bfloat16)
        out[:, heads * head_size :] = summed[:, heads * head_size :].astype(jnp.bfloat16)


def rotate(key_gain, cosine, sine, keep, crossed):
    _, count, width = keep.shape
    result = jax.ShapeDtypeStruct((count, width), jnp.bfloat16)
    return pl.pallas_call(
        rotate_kernel,
        out_shape=(result, result),
        in_specs=[VMEM] * 5,
        out_specs=(VMEM, VMEM),
        compiler_params=pltpu.CompilerParams(vmem_limit_bytes=8 * 1024 * 1024),
        cost_estimate=QUICK,
        name="rotate",
    )(key_gain.reshape(1, -1), cosine, sine, keep, crossed)


def cached_kernel(lengths, q_ref, k_ref, v_ref, out_ref, level_ref):
    filled = lengths[pl.program_id(0)]
    groups, slots, head_size = k_ref.shape
    new_rows, qheads, _ = q_ref.shape
    share = qheads // groups
    rows = new_rows * share
    scale = 1.0 / (math.sqrt(head_size) * math.log(2.0))
    queries = q_ref[...].astype(jnp.float32)
    inside = lax.broadcasted_iota(jnp.int32, (rows, slots), 1) < filled
    lane = lax.broadcasted_iota(jnp.int32, (rows, 128), 1)
    levels = [jnp.full((rows, 128), MASKED, jnp.float32)] * 2
    for g in range(groups):
        pair, place = g // 2, g % 2
        asked = queries[:, g * share : (g + 1) * share, :].reshape(rows, head_size).astype(jnp.bfloat16)
        scores = lax.dot_general(
            asked, k_ref[g], (((1,), (1,)), ((), ())), preferred_element_type=jnp.float32
        )
        scores = jnp.where(inside, scores * scale, MASKED)
        top = jnp.max(scores, axis=1, keepdims=True)
        expo = jnp.exp2(scores - top)
        total = jnp.sum(expo, axis=1, keepdims=True)
        mixed = jnp.dot(expo.astype(jnp.bfloat16), v_ref[g], preferred_element_type=jnp.float32)
        out_ref[pair, :, place * share : (place + 1) * share, :] = (mixed / total).reshape(new_rows, share, head_size)
        level = top + jnp.log(total) * (1.0 / math.log(2.0))
        levels[place] = jnp.where(lane == 2 * new_rows + pair, level, levels[place])
    for place in range(2):
        level_ref[:, place * share : (place + 1) * share, :] = levels[place].reshape(new_rows, share, 128)


def attend_cached(queries, key_cache, value_cache, cache_lengths):
    sequences, new_rows, qheads, head_size = queries.shape
    _, groups, slots, _ = key_cache.shape
    pairs = groups // 2
    rows = new_rows * qheads // pairs
    cache_spec = pl.BlockSpec((None, groups, slots, head_size), lambda s, n: (s, 0, 0, 0))
    return pl.pallas_call(
        cached_kernel,
        out_shape=(
            jax.ShapeDtypeStruct((sequences, pairs, new_rows, qheads // pairs, head_size), jnp.float32),
            jax.ShapeDtypeStruct((sequences, new_rows, qheads // pairs, 128), jnp.float32),
        ),
        grid_spec=pltpu.PrefetchScalarGridSpec(
            num_scalar_prefetch=1,
            grid=(sequences,),
            in_specs=[
                pl.BlockSpec((None, new_rows, qheads, head_size), lambda s, n: (s, 0, 0, 0)),
                cache_spec,
                cache_spec,
            ],
            out_specs=(
                pl.BlockSpec((None, pairs, new_rows, qheads // pairs, head_size), lambda s, n: (s, 0, 0, 0, 0)),
                pl.BlockSpec((None, new_rows, qheads // pairs, 128), lambda s, n: (s, 0, 0, 0)),
            ),
        ),
        compiler_params=pltpu.CompilerParams(vmem_limit_bytes=16 * 1024 * 1024),
        cost_estimate=pl.CostEstimate(flops=4 * 10**9, bytes_accessed=12 * 2**20, transcendentals=10**6),
        name="attend_cached",
    )(cache_lengths, queries, key_cache, value_cache)


def finish_kernel(lengths, place_ref, kv_ref, q_ref, cached_ref, level_ref, *rest):
    entry_ref, out_ref = rest[-2:]
    live = lengths[pl.program_id(0)]
    which = place_ref[0]
    new_rows, asked_heads, head_size = q_ref.shape
    share = asked_heads // 2
    rows = new_rows * asked_heads
    scale = 1.0 / (math.sqrt(head_size) * math.log(2.0))
    lane = lax.broadcasted_iota(jnp.int32, (rows, 128), 1)
    row = lax.broadcasted_iota(jnp.int32, (rows, 128), 0)
    token = row // asked_heads
    offset = lane - new_rows * ((row // share) % 2)
    causal = jnp.logical_and(offset >= 0, offset <= token)
    stored = lane == 2 * new_rows + which
    padding = jnp.zeros((128 - 2 * new_rows, head_size), jnp.bfloat16)
    entry_ref[:, 0, :] = kv_ref[:, : 2 * head_size]
    entry_ref[:, 1, :] = kv_ref[:, 2 * head_size :]

    def stacked(first):
        left = kv_ref[:, first * head_size : (first + 1) * head_size]
        right = kv_ref[:, (first + 1) * head_size : (first + 2) * head_size]
        return jnp.concatenate([left, right, padding], axis=0)

    scores = lax.dot_general(
        q_ref[...].reshape(rows, head_size),
        stacked(0),
        (((1,), (1,)), ((), ())),
        preferred_element_type=jnp.float32,
    )
    kept = jnp.where(stored, level_ref[...].reshape(rows, 128), MASKED)
    scores = jnp.where(causal, scores * scale, kept)
    expo = jnp.exp2(scores - jnp.max(scores, axis=1, keepdims=True))
    total = jnp.sum(expo, axis=1, keepdims=True)
    share_cached = jnp.sum(jnp.where(stored, expo, 0.0), axis=1, keepdims=True)
    mixed = jnp.dot(expo.astype(jnp.bfloat16), stacked(2), preferred_element_type=jnp.float32)
    mixed = (mixed + share_cached * cached_ref[...].reshape(rows, head_size)) / total
    out_ref[...] = jnp.where(token < live, mixed, 0.0).reshape(q_ref.shape).astype(jnp.bfloat16)


def finish(tool_lengths, which, kv, queries, cached, level, earlier):
    sequences, new_rows, qheads, head_size = queries.shape
    _, pairs, _, _, _ = cached.shape
    heads = qheads // pairs
    width = kv.shape[1]
    query_spec = pl.BlockSpec((None, new_rows, qheads // pairs, head_size), lambda s, n, w: (s, 0, w[0], 0))
    entry_spec = pl.BlockSpec((None, new_rows, 2, width // 2), lambda s, n, w: (s, 0, 0, w[0]))
    return pl.pallas_call(
        finish_kernel,
        out_shape=(
            jax.ShapeDtypeStruct((sequences, new_rows, 2, pairs * width // 2), jnp.bfloat16),
            jax.ShapeDtypeStruct(queries.shape, jnp.bfloat16),
        ),
        grid_spec=pltpu.PrefetchScalarGridSpec(
            num_scalar_prefetch=2,
            grid=(sequences,),
            in_specs=[
                pl.BlockSpec((new_rows, width), lambda s, n, w: (s, 0)),
                query_spec,
                pl.BlockSpec((None, None, new_rows, heads, head_size), lambda s, n, w: (s, w[0], 0, 0, 0)),
                pl.BlockSpec((None, new_rows, heads, 128), lambda s, n, w: (s, 0, 0, 0)),
            ]
            + [ANY] * len(earlier),
            out_specs=(entry_spec, query_spec),
        ),
        input_output_aliases={6 + n: n for n in range(len(earlier))},
        compiler_params=pltpu.CompilerParams(vmem_limit_bytes=12 * 1024 * 1024),
        cost_estimate=QUICK,
        name="finish",
    )(tool_lengths, which.reshape(1), kv, queries, cached, level, *earlier)


def fast_device(
    master,
    gradient,
    first_moment,
    second_moment,
    key_gain,
    hidden,
    queries,
    key_cache,
    value_cache,
    cache_lengths,
    tool_lengths,
):
    sequences, new_rows, model_width = hidden.shape
    head_size = key_cache.shape[3]
    count = sequences * new_rows
    tokens = hidden.reshape(count, model_width)
    x = lax.axis_index("role") // 2
    depth = model_width // lax.axis_size("role")

    (updated, moment_one, moment_two), quarters = adam_step(master, gradient, first_moment, second_moment)
    own = quarters[0]
    from_x = lax.ppermute(quarters[1], "role", X_SWAP)
    from_y = lax.ppermute(quarters[2], "tp", TP_SWAP)
    from_xy = lax.ppermute(quarters[3], ("role", "tp"), XY_SWAP)
    near_cut, far_cut, core_cut = cut(hold(tokens, own), depth)
    own = hold(own, near_cut)
    far_own, near_own, middle_own = (lax.ppermute(own, "fsdp", pairs) for pairs in (Z_FAR, Z_NEAR, Z_MIDDLE))
    near_x = lax.ppermute(near_cut, "role", X_SWAP)
    rest = jnp.stack(hold((from_x, from_y, from_xy), far_own, near_own, middle_own))
    far_rest = lax.ppermute(rest, "fsdp", Z_FAR)
    near_rest = lax.ppermute(rest, "fsdp", Z_NEAR)
    far_x = lax.ppermute(hold(far_cut, rest), "role", DIAGONAL)
    crossed_tokens = lax.ppermute(hold(core_cut, rest), "role", CORE_SWAP)
    cached, level = attend_cached(queries, key_cache, value_cache, hold(cache_lengths, rest))
    near_y = lax.ppermute(hold(near_x, level), "tp", TP_SWAP)
    far_y = lax.ppermute(hold(far_x, level), "tp", TP_SWAP)
    ends_own = lax.ppermute(hold(far_own, level), "fsdp", Z_ENDS)
    ready = (far_rest, near_rest, near_y, ends_own)
    ends_rest = lax.ppermute(hold(far_rest, *ready), "fsdp", Z_ENDS)
    middle_rest = lax.ppermute(hold(rest, *ready), "fsdp", Z_MIDDLE)
    lengths_x = lax.ppermute(hold(cache_lengths, *ready), "role", X_SWAP)

    lengths = jnp.stack([cache_lengths, lengths_x])
    positions = (lengths[:, :, None] + jnp.arange(new_rows, dtype=jnp.int32)[None, None, :]).reshape(2, count)
    half = head_size // 2
    inverse = rope_theta ** (-(jnp.arange(half, dtype=jnp.float32) * 2.0) / head_size)
    angles = positions.astype(jnp.float32)[:, :, None] * inverse[None, None, :]
    cosine, sine = jnp.cos(angles), jnp.sin(angles)
    cosine = jnp.concatenate([cosine, cosine], axis=2)
    sine = jnp.concatenate([-sine, sine], axis=2)

    parts = hold((crossed_tokens, near_x, near_y, far_x, far_y), cosine, sine)
    units = (own, rest, near_own, near_rest, far_own, far_rest, middle_own, middle_rest, ends_own, ends_rest)
    keep, send = project(tokens, parts, units)
    crossed = lax.ppermute(send, "role", CORE_SWAP)
    own_kv, sent_kv = rotate(key_gain, cosine, sine, keep, crossed)
    arrived_kv = lax.ppermute(sent_kv, "role", X_SWAP)
    partial = finish(tool_lengths, x, own_kv, queries, cached, level, ())
    new_entries, attended = finish(tool_lengths, 1 - x, arrived_kv, queries, cached, level, partial)
    return (updated, moment_one, moment_two, new_entries, attended)


def device_program(mesh):
    sizes = (mesh.shape["role"], mesh.shape["fsdp"], mesh.shape["tp"])
    return fast_device if sizes == (4, 4, 2) else plain_device


def solution(mesh):
    return jax.shard_map(
        device_program(mesh),
        mesh=mesh,
        in_specs=(
            P(("role", "fsdp", "tp"), None, None),
            P(("role", "fsdp", "tp"), None, None),
            P(("role", "fsdp", "tp"), None, None),
            P(("role", "fsdp", "tp"), None, None),
            P(),
            P(("role", "fsdp"), None, None),
            P(("role", "fsdp"), None, "tp", None),
            P(("role", "fsdp"), "tp", None, None),
            P(("role", "fsdp"), "tp", None, None),
            P(("role", "fsdp")),
            P(("role", "fsdp")),
        ),
        out_specs=(
            P(("role", "fsdp", "tp"), None, None),
            P(("role", "fsdp", "tp"), None, None),
            P(("role", "fsdp", "tp"), None, None),
            P(("role", "fsdp"), None, None, "tp"),
            P(("role", "fsdp"), None, "tp", None),
        ),
        check_vma=False,
    )
```
